32 devices in a mesh: ctx: 8 (over y, x, core), ch: 4 (over z).
Axes of the slice: x: 2, y: 2, z: 4, core: 2. Of those that a mesh axis runs over, the one named last changes fastest.
Arguments:
- projected: bfloat16 [3, 4096, 8192], P(None, 'ctx', 'ch'), may hold values from -6 to 6
- short_weight: float32 [3, 3, 8192], P(None, None, 'ch'), may hold values from -3 to 3
- rates: float32 [16, 8192], P(None, 'ch'), may hold values from 6.1035156e-05 to 0.05
- residues: float32 [16, 8192], P(None, 'ch'), may hold values from -1.5 to 1.5
- bias: float32 [8192], P('ch'), may hold values from -3 to 3
- out_weight: bfloat16 [8192, 8192], P('ch', 'ctx'), may hold values from -0.0625 to 0.0625
Outputs:
- layer_out: bfloat16 [4096, 8192], P('ctx', 'ch')
The draws below stay inside these ranges and needn't reach their ends.
All inputs are finite; a program needn't handle non-finite values.
Results may differ from the reference program's by a relative error of at most 0.018.
Values may be sent and summed in bfloat16 or wider, within the bound.
No kernel may reach another device: no remote copies, remote signals or barrier semaphores. Data moves between devices by JAX's collectives and lax.ppermute only.
A program may use at most 192 MiB of HBM per device.

```python
import math
import jax
import jax.numpy as jnp
from jax import lax

D = 8192
ORDER = 16
SEQ = 4096
N_CH = 4


def level_of(rng, extent, split, low, top_value):
    loudness, own = 1.0, jax.random.fold_in(rng, 6)
    for axis_at, parts in split:
        heights = jnp.exp(jax.random.uniform(jax.random.fold_in(own, axis_at), (parts,), jnp.float32, low / len(split), top_value / len(split)))
        loudness = loudness * jnp.repeat(heights, extent[axis_at] // parts).reshape([-1 if axis == axis_at else 1 for axis in range(len(extent))])
    return loudness


def scatter_about(rng, shape, scale, reach, cuts=(), kind=jnp.bfloat16):
    factor_of = level_of(rng, shape, cuts, -0.22, 0.18) if cuts else 1.0
    result = jax.random.normal(rng, shape, jnp.float32) * scale * factor_of
    return jnp.minimum(jnp.maximum(result, -reach), reach).astype(kind)


def setup_inputs(seed: int = 0) -> dict:
    key_list = jax.random.split(jax.random.key(seed), 7)
    projected = scatter_about(key_list[0], (3, SEQ, D), 1.0, 6.0, ((1, 8), (2, 4)))
    short_weight = scatter_about(key_list[1], (3, 3, D), 0.6, 3.0, ((2, 4),), jnp.float32)
    rates = jnp.clip(jnp.exp(math.log(0.05) - 6.7083283 * jax.random.uniform(key_list[2], (ORDER, D), jnp.float32) ** level_of(key_list[2], (ORDER, D), ((1, 4),), -0.2, 0.2)), 6.103515625e-05, 0.05)
    residues = scatter_about(key_list[3], (ORDER, D), 0.25, 1.5, ((1, 4),), jnp.float32)
    bias = scatter_about(key_list[4], (D,), 0.5, 3.0, ((0, 4),), jnp.float32)
    out_weight = scatter_about(key_list[5], (D, D), D ** -0.5, 0.0625, ((0, 4), (1, 8)))
    return {"projected": projected, "short_weight": short_weight, "rates": rates, "residues": residues, "bias": bias, "out_weight": out_weight}


def long_conv(args):
    values, decay, coef = args
    total = values.shape[0]
    steps = jnp.arange(total, dtype=jnp.float32)
    filt = lax.optimization_barrier(jnp.sum(coef[None] * jnp.exp(-decay[None] * steps[:, None, None]), axis=1))
    length = 2 * total
    spectrum = jnp.fft.rfft(values, length, axis=0) * jnp.fft.rfft(filt, length, axis=0)
    return jnp.fft.irfft(spectrum, length, axis=0)[:total]

def reference(projected, short_weight, rates, residues, bias, out_weight):
    total = projected.shape[1]
    width = projected.shape[2]
    inputs = projected.astype(jnp.float32)
    padded = jnp.pad(inputs, ((0, 0), (2, 0), (0, 0)))
    short = short_weight[:, 0, None, :] * padded[:, 2:2 + total, :]
    short = short + short_weight[:, 1, None, :] * padded[:, 1:1 + total, :]
    short = short + short_weight[:, 2, None, :] * padded[:, 0:total, :]
    gated = (short[1] * short[2]).astype(jnp.bfloat16)
    values = gated.astype(jnp.float32)
    group = math.gcd(width, 256)
    count = width // group
    coef = residues * jnp.sqrt(2.0 * rates)
    grouped = values.reshape(total, count, group).transpose(1, 0, 2)
    decay_groups = rates.reshape(ORDER, count, group).transpose(1, 0, 2)
    coef_groups = coef.reshape(ORDER, count, group).transpose(1, 0, 2)
    conv = lax.map(long_conv, (grouped, decay_groups, coef_groups))
    conv = conv.transpose(1, 0, 2).reshape(total, width)
    conv = conv + bias[None, :] * values
    mixed = (short[0] * conv).astype(jnp.bfloat16)
    per_group = width // N_CH
    summed = jnp.zeros((total, width), jnp.float32)
    for index in range(N_CH):
        lower = index * per_group
        partial_value = jnp.dot(mixed[:, lower:lower + per_group], out_weight[lower:lower + per_group, :], preferred_element_type=jnp.float32)
        summed = summed + partial_value.astype(jnp.bfloat16).astype(jnp.float32)
    return summed.astype(jnp.bfloat16)
```

```python
import functools

import jax
import jax.numpy as jnp
from jax import lax
from jax.experimental import pallas as pl
from jax.experimental.pallas import tpu as pltpu
from jax.sharding import PartitionSpec as P

F32 = jnp.float32
BF16 = jnp.bfloat16
TILES = 4
SUB = 8
LANES = 128
CUTS = 4
VMEM = 63 * 1024 * 1024
SMEM_SPEC = pl.BlockSpec(memory_space=pltpu.SMEM)
ANY_SPEC = pl.BlockSpec(memory_space=pl.ANY)


def swap(value, axis, mask):
    count = lax.axis_size(axis)
    return lax.ppermute(value, axis, [(i, i ^ mask) for i in range(count)])


def from_behind(value, axis):
    count = lax.axis_size(axis)
    return lax.ppermute(value, axis, [(i, i + 1) for i in range(count - 1)])


def spread(row):
    return jnp.broadcast_to(row, (SUB, LANES))


def total(parts):
    parts = list(parts)
    while len(parts) > 1:
        parts = [
            parts[i] + parts[i + 1] if i + 1 < len(parts) else parts[i]
            for i in range(0, len(parts), 2)
        ]
    return parts[0]


def rounded(value):
    return value.astype(BF16).astype(F32)


def cost(micros, moved):
    return pl.CostEstimate(flops=int(micros * 1.0e9), bytes_accessed=int(moved), transcendentals=0)


def params():
    return pltpu.CompilerParams(vmem_limit_bytes=VMEM)


def local_kernel(
    k_ref, v_ref, halo_ref, taps_ref, rates_ref, coef_ref, bias_ref, after_ref,
    y_ref, entry_ref, end_ref, k_rows, v_rows, ends,
):
    rows, width = k_ref.shape[1], k_ref.shape[2]
    order = rates_ref.shape[0]
    length = rows // SUB
    unroll = min(8, length)
    sub = lax.broadcasted_iota(jnp.int32, (SUB, LANES), 0)

    def group(index, _):
        lanes = pl.ds(pl.multiple_of(index * LANES, LANES), LANES)
        k_rows[pl.ds(SUB - 2, 2), :] = halo_ref[1, :, lanes].astype(F32)
        v_rows[pl.ds(SUB - 2, 2), :] = halo_ref[2, :, lanes].astype(F32)
        k_rows[pl.ds(SUB, rows), :] = k_ref[0, :, lanes].astype(F32)
        v_rows[pl.ds(SUB, rows), :] = v_ref[0, :, lanes].astype(F32)
        decay = [spread(jnp.exp(-rates_ref[m : m + 1, lanes])) for m in range(order)]
        coef = [spread(coef_ref[m : m + 1, lanes]) for m in range(order)]
        bias = spread(bias_ref[0:1, lanes])
        kt = [spread(taps_ref[1, j : j + 1, lanes]) for j in range(3)]
        vt = [spread(taps_ref[2, j : j + 1, lanes]) for j in range(3)]

        def pick(ref, b):
            return ref[pl.ds(SUB + b, SUB, stride=length), :]

        def steps(outer, carry):
            k1, k2, v1, v2, state = carry
            for u in range(unroll):
                b = outer * unroll + u
                k0, v0 = pick(k_rows, b), pick(v_rows, b)
                short_k = kt[0] * k0 + kt[1] * k1 + kt[2] * k2
                short_v = vt[0] * v0 + vt[1] * v1 + vt[2] * v2
                gated = rounded(short_k * short_v)
                state = [decay[m] * state[m] + coef[m] * gated for m in range(order)]
                y_ref[b, :, lanes] = total(state + [bias * gated])
                k1, k2, v1, v2 = k0, k1, v0, v1
            return k1, k2, v1, v2, state

        zero = jnp.zeros((SUB, LANES), F32)
        start = (pick(k_rows, -1), pick(k_rows, -2), pick(v_rows, -1), pick(v_rows, -2), [zero] * order)
        state = lax.fori_loop(0, length // unroll, steps, start)[4]
        for m in range(order):
            rate = spread(rates_ref[m : m + 1, lanes])
            scan = state[m]
            reach = 1
            while reach < SUB:
                earlier = pltpu.roll(scan, reach, 0) * jnp.exp(-rate * float(length * reach))
                scan = scan + jnp.where(sub >= reach, earlier, 0.0)
                reach *= 2
            entry_ref[m, :, lanes] = jnp.where(sub >= 1, pltpu.roll(scan, 1, 0), 0.0)
            ends[m : m + 1, :] = scan[SUB - 1 :, :]
        end_ref[:, lanes] = ends[...].astype(end_ref.dtype)
        return 0

    lax.fori_loop(0, width // LANES, group, 0)


def local_part(projected, halo, taps, rates, coef, bias, after):
    rows, width = projected.shape[1:]
    order = rates.shape[0]
    tile = width // TILES
    length = rows // SUB
    return pl.pallas_call(
        local_kernel,
        grid=(width // tile,),
        in_specs=[
            pl.BlockSpec((1, rows, tile), lambda c: (1, 0, c)),
            pl.BlockSpec((1, rows, tile), lambda c: (2, 0, c)),
            pl.BlockSpec((3, 2, tile), lambda c: (0, 0, c)),
            pl.BlockSpec((3, 3, tile), lambda c: (0, 0, c)),
            pl.BlockSpec((order, tile), lambda c: (0, c)),
            pl.BlockSpec((order, tile), lambda c: (0, c)),
            pl.BlockSpec((1, tile), lambda c: (0, c)),
            ANY_SPEC,
        ],
        out_specs=[
            pl.BlockSpec((length, SUB, tile), lambda c: (0, 0, c)),
            pl.BlockSpec((order, SUB, tile), lambda c: (0, 0, c)),
            pl.BlockSpec((order, tile), lambda c: (0, c)),
        ],
        out_shape=[
            jax.ShapeDtypeStruct((length, SUB, width), F32),
            jax.ShapeDtypeStruct((order, SUB, width), F32),
            jax.ShapeDtypeStruct((order, width), BF16),
        ],
        scratch_shapes=[
            pltpu.VMEM((rows + SUB, LANES), F32),
            pltpu.VMEM((rows + SUB, LANES), F32),
            pltpu.VMEM((order, LANES), F32),
        ],
        compiler_params=params(),
        cost_estimate=cost(20, 12 * rows * width),
        name="local_conv",
    )(projected, projected, halo, taps, rates, coef, bias, after)


def mix_kernel(
    count, mine_ref, q_ref, halo_ref, taps_ref, rates_ref, y_ref, entry_ref, ends_ref, *refs
):
    outs, (q_rows, mixed_rows) = refs[-2 - count : -2], refs[-2:]
    rows, width = q_ref.shape[1], q_ref.shape[2]
    order = rates_ref.shape[0]
    length = rows // SUB
    unroll = min(8, length)
    sub = lax.broadcasted_iota(jnp.int32, (SUB, LANES), 0).astype(F32)

    def group(index, _):
        lanes = pl.ds(pl.multiple_of(index * LANES, LANES), LANES)
        rates = rates_ref[:, lanes]
        across = jnp.exp(-rates * float(rows))
        before = jnp.zeros((order, LANES), F32)
        for device in range(ends_ref.shape[0] - 1):
            later = before * across + ends_ref[device, :, lanes].astype(F32)
            before = jnp.where(device < mine_ref[0], later, before)
        q_rows[pl.ds(SUB - 2, 2), :] = halo_ref[0, :, lanes].astype(F32)
        q_rows[pl.ds(SUB, rows), :] = q_ref[0, :, lanes].astype(F32)
        decay, carried = [], []
        for m in range(order):
            rate = spread(rates[m : m + 1, :])
            decay.append(jnp.exp(-rate))
            at_entry = entry_ref[m, :, lanes] + spread(before[m : m + 1, :]) * jnp.exp(
                -rate * (sub * float(length))
            )
            carried.append(at_entry * decay[m])
        qt = [spread(taps_ref[0, j : j + 1, lanes]) for j in range(3)]

        def pick(b):
            return q_rows[pl.ds(SUB + b, SUB, stride=length), :]

        def steps(outer, carry):
            q1, q2, carried = carry
            for u in range(unroll):
                b = outer * unroll + u
                q0 = pick(b)
                short_q = qt[0] * q0 + qt[1] * q1 + qt[2] * q2
                conv = y_ref[b, :, lanes] + total(carried)
                mixed_rows[pl.ds(b, SUB, stride=length), :] = short_q * conv
                carried = [carried[m] * decay[m] for m in range(order)]
                q1, q2 = q0, q1
            return q1, q2, carried

        lax.fori_loop(0, length // unroll, steps, (pick(-1), pick(-2), carried))
        for step, out in enumerate(outs):

            @pl.when(pl.program_id(0) == step)
            def _():
                out[:, lanes] = mixed_rows[...].astype(out.dtype)

        return 0

    lax.fori_loop(0, width // LANES, group, 0)


def mix_part(mine, projected, halo, taps, rates, y, entry, ends, tiles, after):
    rows, width = projected.shape[1:]
    order = rates.shape[0]
    tile = width // TILES
    length = rows // SUB
    first, count = tiles[0], len(tiles)
    return pl.pallas_call(
        functools.partial(mix_kernel, count),
        grid=(count,),
        in_specs=[
            SMEM_SPEC,
            pl.BlockSpec((1, rows, tile), lambda c: (0, 0, first + c)),
            pl.BlockSpec((3, 2, tile), lambda c: (0, 0, first + c)),
            pl.BlockSpec((3, 3, tile), lambda c: (0, 0, first + c)),
            pl.BlockSpec((order, tile), lambda c: (0, first + c)),
            pl.BlockSpec((length, SUB, tile), lambda c: (0, 0, first + c)),
            pl.BlockSpec((order, SUB, tile), lambda c: (0, 0, first + c)),
            pl.BlockSpec((ends.shape[0], order, tile), lambda c: (0, 0, first + c)),
        ] + [ANY_SPEC] * len(after),
        out_specs=[pl.BlockSpec((rows, tile), lambda c: (0, 0))] * count,
        out_shape=[jax.ShapeDtypeStruct((rows, tile), BF16)] * count,
        scratch_shapes=[
            pltpu.VMEM((rows + SUB, LANES), F32),
            pltpu.VMEM((rows, LANES), F32),
        ],
        compiler_params=params(),
        cost_estimate=cost(20, 8),
        name="mix",
    )(mine, projected, halo, taps, rates, y, entry, ends, *after)


def join_kernel(*refs):
    pass


def join_part(value, after):
    return pl.pallas_call(
        join_kernel,
        in_specs=[ANY_SPEC] * (1 + len(after)),
        out_specs=ANY_SPEC,
        out_shape=jax.ShapeDtypeStruct(value.shape, value.dtype),
        input_output_aliases={0: 0},
        cost_estimate=cost(0.1, 8),
        name="join",
    )(value, *after)


def copy_kernel(places, *refs):
    count = len(places)
    outs, stages, sems = refs[-2 * count - 1 : -count - 1], refs[-count - 1 : -1], refs[-1]
    moves = []
    for i, (rows, cols) in enumerate(places):
        size = rows[1] // CUTS
        for j in range(CUTS):
            here = pl.ds(j * size, size)
            there = refs[i].at[pl.ds(rows[0] + j * size, size), pl.ds(*cols)]
            moves.append((
                pltpu.make_async_copy(there, stages[i].at[here], sems.at[0, i, j]),
                pltpu.make_async_copy(stages[i].at[here], outs[i].at[here], sems.at[1, i, j]),
            ))
    for load, _ in moves:
        load.start()
    for load, store in moves:
        load.wait()
        store.start()
    for _, store in moves:
        store.wait()


def copy_part(sources, after, name):
    arrays = [array for array, _, _ in sources]
    places = [(rows, cols) for _, rows, cols in sources]
    out_shape = [jax.ShapeDtypeStruct((rows[1], cols[1]), a.dtype) for a, rows, cols in sources]
    return pl.pallas_call(
        functools.partial(copy_kernel, places),
        in_specs=[ANY_SPEC] * (len(arrays) + len(after)),
        out_specs=[ANY_SPEC] * len(out_shape),
        out_shape=out_shape,
        scratch_shapes=[pltpu.VMEM((rows[1], cols[1]), a.dtype) for a, rows, cols in sources]
        + [pltpu.SemaphoreType.DMA((2, len(sources), CUTS))],
        compiler_params=params(),
        cost_estimate=cost(0.1, 8),
        name=name,
    )(*arrays, *after)


def project_kernel(parts, slot_ref, *refs):
    sides = [
        jnp.concatenate([ref[...] for ref in refs[side * TILES : (side + 1) * TILES]], axis=1)
        for side in range(2)
    ]
    refs = refs[2 * TILES :]
    weights, (after_ref, out_ref, token_ref) = refs[: sum(parts)], refs[sum(parts) :]
    token_ref[...] = jnp.zeros(token_ref.shape, F32)
    at = 0
    for piece, count in enumerate(parts):
        for side, tokens in enumerate(sides):
            result = None
            low = 0
            for part in weights[at : at + count]:
                depth = part.shape[0]
                term = jnp.dot(tokens[:, low : low + depth], part[...], preferred_element_type=F32)
                result = term if result is None else result + term
                low += depth
            out_ref[piece ^ slot_ref[0], side] = result.astype(BF16)
        at += count


def project_part(slot, own, other, pieces, first, width, weight, after):
    rows, depth = own[0].shape
    parts = [len(piece) for piece in pieces]
    weights = [part for piece in pieces for part in piece]
    steps = 2
    tile = rows // steps
    in_specs = [SMEM_SPEC] + [pl.BlockSpec((tile, depth), lambda i: (i, 0))] * (2 * TILES)
    for i, part in enumerate(weights):
        if i == 0:
            in_specs.append(
                pl.BlockSpec((pl.Element(part.shape[0]), pl.Element(width)), lambda i: (0, first))
            )
        else:
            in_specs.append(pl.BlockSpec(part.shape, lambda i: (0, 0)))
    count = len(pieces)
    return pl.pallas_call(
        functools.partial(project_kernel, parts),
        grid=(steps,),
        in_specs=in_specs + [ANY_SPEC],
        out_specs=[
            pl.BlockSpec((count, 2, tile, width), lambda i: (0, 0, i, 0)),
            pl.BlockSpec((SUB, LANES), lambda i: (0, 0)),
        ],
        out_shape=[
            jax.ShapeDtypeStruct((count, 2, rows, width), BF16),
            jax.ShapeDtypeStruct((SUB, LANES), F32),
        ],
        compiler_params=params(),
        cost_estimate=cost(weight, 8),
        name="project",
    )(slot, *own, *other, *weights, after)


def place_kernel(side_ref, *refs):
    refs[-1][...] = refs[0][...]


def place_both_kernel(side_ref, sums_ref, *refs):
    refs[-2][...] = sums_ref[0]
    refs[-1][...] = sums_ref[1]


def place_part(side, sums, landed, first, out, shape):
    rows, half = shape[0], shape[1] // 2 // LANES
    strip = sums if landed is None else landed
    width = strip.shape[-1]

    def column(i, side_ref):
        which = side_ref[0] if landed is None else 1 - side_ref[0]
        return (0, which * half + first // LANES + i)

    if landed is None:
        in_specs = [pl.BlockSpec((2, rows, LANES), lambda i, side_ref: (0, 0, i))]
    else:
        in_specs = [pl.BlockSpec((rows, LANES), lambda i, side_ref: (0, i))]
    out_specs = [pl.BlockSpec((rows, LANES), column)]
    out_shape = [jax.ShapeDtypeStruct(shape, BF16)]
    if landed is None:
        out_specs.append(pl.BlockSpec((rows, LANES), lambda i, side_ref: (0, i)))
        out_shape.append(jax.ShapeDtypeStruct((rows, width), BF16))
    args, aliases = [strip], {}
    if out is not None:
        aliases = {2: 0}
        in_specs.append(ANY_SPEC)
        args.append(out)
    return pl.pallas_call(
        place_both_kernel if landed is None else place_kernel,
        grid_spec=pltpu.PrefetchScalarGridSpec(
            num_scalar_prefetch=1,
            grid=(width // LANES,),
            in_specs=in_specs,
            out_specs=out_specs,
        ),
        out_shape=out_shape,
        input_output_aliases=aliases,
        compiler_params=params(),
        cost_estimate=cost(0.2, 8),
        name="place",
    )(side, *args)


def body(projected, short_weight, rates, residues, bias, out_weight):
    rows, width = projected.shape[1:]
    depth, columns = out_weight.shape
    count = lax.axis_size("ctx")
    groups = lax.axis_size("ch")
    per = count // groups
    assert per == 2
    mine = lax.axis_index("ctx")
    slot = ((mine // per) ^ lax.axis_index("ch")).astype(jnp.int32)[None]
    coef = residues * jnp.sqrt(2.0 * rates)
    near, far = 2, 4
    more = [1 << b for b in range(3, 16) if 1 << b < count]

    units = columns // LANES
    first = max(units // 4, 1)
    second = (units - first + 1) // 2
    widths = [LANES * part for part in (first, second, units - first - second)]
    starts = [sum(widths[:s]) for s in range(len(widths))]
    stages = len(widths)

    def cut_of(s):
        return (out_weight, (0, depth), (starts[s], widths[s]))

    def first_hops(sent):
        return swap(sent, "ctx", near), swap(sent, "ctx", far)

    def second_hops(s, arrived, after, then=True):
        half, cols = depth // 2, (0, widths[s])
        sources = [(arrived[0], (0, half), cols), (arrived[1], (half, half), cols)]
        if then and s + 1 < stages:
            sources.append(cut_of(s + 1))
        low, high, *sent = copy_part(sources, after, "pass_weights")
        diagonal = [swap(low, "ctx", far), swap(high, "ctx", near)]
        return low, diagonal, first_hops(sent[0]) if sent else None

    def pieces_of(s, arrived, diagonal):
        pieces = {
            0: [out_weight],
            near: [arrived[0]],
            far: [arrived[1]],
            near | far: list(diagonal),
        }
        for mask in more:
            for r, parts in list(pieces.items()):
                if r == 0:
                    parts = [out_weight[:, starts[s] : starts[s] + widths[s]]]
                pieces[r ^ mask] = [swap(part, "ctx", mask) for part in parts]
        return [pieces[r] for r in sorted(pieces)]

    halo = from_behind(projected[:, rows - 2 :, :], "ctx")
    (sent,) = copy_part([cut_of(0)], [halo], "cut")
    arrived = first_hops(sent)
    y, entry, end = local_part(projected, halo, short_weight, rates, coef, bias[None], sent)
    ends = lax.all_gather(join_part(end, arrived), "ctx")
    token, diagonal, _ = second_hops(0, arrived, [ends], then=False)
    mixed, other = [], []
    for tiles in (range(TILES // 2), range(TILES // 2, TILES)):
        made = mix_part(
            mine.astype(jnp.int32)[None], projected, halo, short_weight, rates, y, entry, ends, tiles,
            [token, *(diagonal if mixed else ())],
        )
        if not mixed:
            (token,) = copy_part([cut_of(1)], [made[0]], "cut")
            upcoming = first_hops(token)
        mixed += made
        other += [swap(part, "ctx", 1) for part in made]
    token = mixed[-1]
    slot = (mine // per).astype(jnp.int32)[None]
    side = (mine % per).astype(jnp.int32)[None]
    shape = (rows, per * columns)
    sums = []

    def place_stage(s, out):
        out, given = place_part(side, sums[s], None, starts[s], out, shape)
        return place_part(side, None, swap(given, "ctx", 1), starts[s], out, shape)[0]

    for s in range(stages):
        if s > 0:
            arrived = upcoming
            token, diagonal, upcoming = second_hops(s, arrived, [token, *sums[: s - 1]])
        pieces = pieces_of(s, arrived, diagonal)
        partial, token = project_part(
            slot, mixed, other, pieces, starts[s], widths[s], (0.1, 35, 50)[s], token
        )
        if s == stages - 1:
            out = place_stage(0, None)
            partial = join_part(partial, [sums[-1], out])
        elif s > 0:
            partial = join_part(partial, sums[-1:])
        sums.append(lax.psum_scatter(partial, "ch", scatter_dimension=0))
    for s in range(1, stages):
        out = place_stage(s, out)
    return out


def solution(mesh):
    in_specs = (
        P(None, "ctx", "ch"),
        P(None, None, "ch"),
        P(None, "ch"),
        P(None, "ch"),
        P("ch"),
        P("ch", "ctx"),
    )
    out_specs = P("ctx", "ch")
    return jax.shard_map(body, mesh=mesh, in_specs=in_specs, out_specs=out_specs, check_vma=False)
```

```python
import functools

import jax
import jax.numpy as jnp
from jax import lax
from jax.experimental import pallas as pl
from jax.experimental.pallas import tpu as pltpu
from jax.sharding import PartitionSpec as P

F32 = jnp.float32
BF16 = jnp.bfloat16
STEPS = 2
TILES = 4
REACHES = (1, 2, 4)
SUB = 8
LANES = 128
CUTS = 4
K1COST = 60
MIXCOST = 20
PA, PB, PC = 0.1, 35, 50
VMEM = 63 * 1024 * 1024
SMEM_SPEC = pl.BlockSpec(memory_space=pltpu.SMEM)
ANY_SPEC = pl.BlockSpec(memory_space=pl.ANY)


def swap(value, axis, mask):
    count = lax.axis_size(axis)
    return lax.ppermute(value, axis, [(i, i ^ mask) for i in range(count)])


def from_behind(value, axis):
    count = lax.axis_size(axis)
    return lax.ppermute(value, axis, [(i, i + 1) for i in range(count - 1)])


def spread(row):
    return jnp.broadcast_to(row, (SUB, LANES))


def total(parts):
    parts = list(parts)
    while len(parts) > 1:
        parts = [
            parts[i] + parts[i + 1] if i + 1 < len(parts) else parts[i]
            for i in range(0, len(parts), 2)
        ]
    return parts[0]


def rounded(value):
    return value.astype(BF16).astype(F32)


def cost(micros, moved):
    return pl.CostEstimate(flops=int(micros * 1.0e9), bytes_accessed=int(moved), transcendentals=0)


def params():
    return pltpu.CompilerParams(vmem_limit_bytes=VMEM)


def local_kernel(
    k_ref, v_ref, halo_ref, taps_ref, rates_ref, residues_ref, bias_ref, after_ref,
    y_ref, entry_ref, end_ref, k_rows, v_rows, ends,
):
    rows, width = k_ref.shape[1], k_ref.shape[2]
    order = rates_ref.shape[0]
    length = rows // SUB
    unroll = min(8, length)
    sub = lax.broadcasted_iota(jnp.int32, (SUB, LANES), 0)

    def group(index, _):
        lanes = pl.ds(pl.multiple_of(index * LANES, LANES), LANES)
        k_rows[pl.ds(SUB - 2, 2), :] = halo_ref[1, :, lanes].astype(F32)
        v_rows[pl.ds(SUB - 2, 2), :] = halo_ref[2, :, lanes].astype(F32)
        k_rows[pl.ds(SUB, rows), :] = k_ref[0, :, lanes].astype(F32)
        v_rows[pl.ds(SUB, rows), :] = v_ref[0, :, lanes].astype(F32)
        rates = rates_ref[:, lanes]
        all_decay = jnp.exp(-rates)
        all_coef = residues_ref[:, lanes] * jnp.sqrt(2.0 * rates)
        decay = [spread(all_decay[m : m + 1, :]) for m in range(order)]
        coef = [spread(all_coef[m : m + 1, :]) for m in range(order)]
        bias = spread(bias_ref[0:1, lanes])
        kt = [spread(taps_ref[1, j : j + 1, lanes]) for j in range(3)]
        vt = [spread(taps_ref[2, j : j + 1, lanes]) for j in range(3)]

        def pick(ref, b):
            return ref[pl.ds(SUB + b, SUB, stride=length), :]

        def steps(outer, carry):
            k1, k2, v1, v2, state = carry
            for u in range(unroll):
                b = outer * unroll + u
                k0, v0 = pick(k_rows, b), pick(v_rows, b)
                short_k = kt[0] * k0 + kt[1] * k1 + kt[2] * k2
                short_v = vt[0] * v0 + vt[1] * v1 + vt[2] * v2
                gated = rounded(short_k * short_v)
                state = [decay[m] * state[m] + coef[m] * gated for m in range(order)]
                y_ref[b, :, lanes] = total(state + [bias * gated])
                k1, k2, v1, v2 = k0, k1, v0, v1
            return k1, k2, v1, v2, state

        zero = jnp.zeros((SUB, LANES), F32)
        start = (pick(k_rows, -1), pick(k_rows, -2), pick(v_rows, -1), pick(v_rows, -2), [zero] * order)
        state = lax.fori_loop(0, length // unroll, steps, start)[4]
        leaps = {reach: jnp.exp(rates * float(-length * reach)) for reach in REACHES}
        for m in range(order):
            scan = state[m]
            for reach in REACHES:
                earlier = pltpu.roll(scan, reach, 0) * spread(leaps[reach][m : m + 1, :])
                scan = scan + jnp.where(sub >= reach, earlier, 0.0)
            entry_ref[m, :, lanes] = jnp.where(sub >= 1, pltpu.roll(scan, 1, 0), 0.0)
            ends[m : m + 1, :] = scan[SUB - 1 :, :]
        end_ref[:, lanes] = ends[...].astype(end_ref.dtype)
        return 0

    lax.fori_loop(0, width // LANES, group, 0)


def local_part(projected, halo, taps, rates, residues, bias, after):
    rows, width = projected.shape[1:]
    order = rates.shape[0]
    tile = width // TILES
    length = rows // SUB
    return pl.pallas_call(
        local_kernel,
        grid=(width // tile,),
        in_specs=[
            pl.BlockSpec((1, rows, tile), lambda c: (1, 0, c)),
            pl.BlockSpec((1, rows, tile), lambda c: (2, 0, c)),
            pl.BlockSpec((3, 2, tile), lambda c: (0, 0, c)),
            pl.BlockSpec((3, 3, tile), lambda c: (0, 0, c)),
            pl.BlockSpec((order, tile), lambda c: (0, c)),
            pl.BlockSpec((order, tile), lambda c: (0, c)),
            pl.BlockSpec((1, tile), lambda c: (0, c)),
            ANY_SPEC,
        ],
        out_specs=[
            pl.BlockSpec((length, SUB, tile), lambda c: (0, 0, c)),
            pl.BlockSpec((order, SUB, tile), lambda c: (0, 0, c)),
            pl.BlockSpec((order, tile), lambda c: (0, c)),
        ],
        out_shape=[
            jax.ShapeDtypeStruct((length, SUB, width), F32),
            jax.ShapeDtypeStruct((order, SUB, width), F32),
            jax.ShapeDtypeStruct((order, width), BF16),
        ],
        scratch_shapes=[
            pltpu.VMEM((rows + SUB, LANES), F32),
            pltpu.VMEM((rows + SUB, LANES), F32),
            pltpu.VMEM((order, LANES), F32),
        ],
        compiler_params=params(),
        cost_estimate=cost(K1COST, 12 * rows * width),
        name="local_conv",
    )(projected, projected, halo, taps, rates, residues, bias, after)


def mix_kernel(
    count, cut, mine_ref, q_ref, halo_ref, taps_ref, rates_ref, y_ref, entry_ref, ends_ref, *refs
):
    outs, (q_rows, mixed_rows) = refs[-2 - count - cut : -2 - cut], refs[-2:]
    if cut:
        refs[-3][...] = refs[0][...]
    rows, width = q_ref.shape[1], q_ref.shape[2]
    order = rates_ref.shape[0]
    length = rows // SUB
    unroll = min(8, length)
    sub = lax.broadcasted_iota(jnp.int32, (SUB, LANES), 0)

    def group(index, _):
        lanes = pl.ds(pl.multiple_of(index * LANES, LANES), LANES)
        rates = rates_ref[:, lanes]
        across = jnp.exp(-rates * float(rows))
        before = jnp.zeros((order, LANES), F32)
        for device in range(ends_ref.shape[0] - 1):
            later = before * across + ends_ref[device, :, lanes].astype(F32)
            before = jnp.where(device < mine_ref[0], later, before)
        q_rows[pl.ds(SUB - 2, 2), :] = halo_ref[0, :, lanes].astype(F32)
        q_rows[pl.ds(SUB, rows), :] = q_ref[0, :, lanes].astype(F32)
        decay, carried = [], []
        all_decay = jnp.exp(-rates)
        leaps = {reach: jnp.exp(rates * float(-length * reach)) for reach in REACHES}
        for m in range(order):
            decay.append(spread(all_decay[m : m + 1, :]))
            passed = spread(before[m : m + 1, :])
            for reach in REACHES:
                passed = jnp.where(sub & reach == 0, passed, passed * spread(leaps[reach][m : m + 1, :]))
            carried.append((entry_ref[m, :, lanes] + passed) * decay[m])
        qt = [spread(taps_ref[0, j : j + 1, lanes]) for j in range(3)]

        def pick(b):
            return q_rows[pl.ds(SUB + b, SUB, stride=length), :]

        def steps(outer, carry):
            q1, q2, carried = carry
            for u in range(unroll):
                b = outer * unroll + u
                q0 = pick(b)
                short_q = qt[0] * q0 + qt[1] * q1 + qt[2] * q2
                conv = y_ref[b, :, lanes] + total(carried)
                mixed_rows[pl.ds(b, SUB, stride=length), :] = short_q * conv
                carried = [carried[m] * decay[m] for m in range(order)]
                q1, q2 = q0, q1
            return q1, q2, carried

        lax.fori_loop(0, length // unroll, steps, (pick(-1), pick(-2), carried))
        for step, out in enumerate(outs):

            @pl.when(pl.program_id(0) == step)
            def _():
                out[:, lanes] = mixed_rows[...].astype(out.dtype)

        return 0

    lax.fori_loop(0, width // LANES, group, 0)


def mix_part(mine, projected, halo, taps, rates, y, entry, ends, tiles, cut, after):
    rows, width = projected.shape[1:]
    order = rates.shape[0]
    tile = width // TILES
    length = rows // SUB
    first, count = tiles[0], len(tiles)
    in_specs = [
        SMEM_SPEC,
        pl.BlockSpec((1, rows, tile), lambda c: (0, 0, first + c)),
        pl.BlockSpec((3, 2, tile), lambda c: (0, 0, first + c)),
        pl.BlockSpec((3, 3, tile), lambda c: (0, 0, first + c)),
        pl.BlockSpec((order, tile), lambda c: (0, first + c)),
        pl.BlockSpec((length, SUB, tile), lambda c: (0, 0, first + c)),
        pl.BlockSpec((order, SUB, tile), lambda c: (0, 0, first + c)),
        pl.BlockSpec((ends.shape[0], order, tile), lambda c: (0, 0, first + c)),
    ]
    out_specs = [pl.BlockSpec((rows, tile), lambda c: (0, 0))] * count
    out_shape = [jax.ShapeDtypeStruct((rows, tile), BF16)] * count
    args = [mine, projected, halo, taps, rates, y, entry, ends]
    if cut:
        w, column, columns = cut
        depth = w.shape[0] // STEPS
        in_specs.append(
            pl.BlockSpec(
                (pl.Element(depth), pl.Element(columns)),
                lambda c: (jnp.minimum(c, STEPS - 1) * depth, column),
            )
        )
        out_specs.append(pl.BlockSpec((depth, columns), lambda c: (jnp.minimum(c, STEPS - 1), 0)))
        out_shape.append(jax.ShapeDtypeStruct((w.shape[0], columns), BF16))
        args.append(w)
    return pl.pallas_call(
        functools.partial(mix_kernel, count, cut is not None),
        grid=(count,),
        in_specs=in_specs + [ANY_SPEC] * len(after),
        out_specs=out_specs,
        out_shape=out_shape,
        scratch_shapes=[
            pltpu.VMEM((rows + SUB, LANES), F32),
            pltpu.VMEM((rows, LANES), F32),
        ],
        compiler_params=params(),
        cost_estimate=cost(MIXCOST, 8),
        name="mix",
    )(*args, *after)


def join_kernel(*refs):
    pass


def join_part(value, after):
    return pl.pallas_call(
        join_kernel,
        in_specs=[ANY_SPEC] * (1 + len(after)),
        out_specs=ANY_SPEC,
        out_shape=jax.ShapeDtypeStruct(value.shape, value.dtype),
        input_output_aliases={0: 0},
        cost_estimate=cost(0.1, 8),
        name="join",
    )(value, *after)


def copy_kernel(places, *refs):
    count = len(places)
    outs, stages, sems = refs[-2 * count - 1 : -count - 1], refs[-count - 1 : -1], refs[-1]
    moves = []
    for i, (rows, cols) in enumerate(places):
        size = rows[1] // CUTS
        for j in range(CUTS):
            here = pl.ds(j * size, size)
            there = refs[i].at[pl.ds(rows[0] + j * size, size), pl.ds(*cols)]
            moves.append((
                pltpu.make_async_copy(there, stages[i].at[here], sems.at[0, i, j]),
                pltpu.make_async_copy(stages[i].at[here], outs[i].at[here], sems.at[1, i, j]),
            ))
    for load, _ in moves:
        load.start()
    for load, store in moves:
        load.wait()
        store.start()
    for _, store in moves:
        store.wait()


def copy_part(sources, after, name):
    arrays = [array for array, _, _ in sources]
    places = [(rows, cols) for _, rows, cols in sources]
    out_shape = [jax.ShapeDtypeStruct((rows[1], cols[1]), a.dtype) for a, rows, cols in sources]
    return pl.pallas_call(
        functools.partial(copy_kernel, places),
        in_specs=[ANY_SPEC] * (len(arrays) + len(after)),
        out_specs=[ANY_SPEC] * len(out_shape),
        out_shape=out_shape,
        scratch_shapes=[pltpu.VMEM((rows[1], cols[1]), a.dtype) for a, rows, cols in sources]
        + [pltpu.SemaphoreType.DMA((2, len(sources), CUTS))],
        compiler_params=params(),
        cost_estimate=cost(0.1, 8),
        name=name,
    )(*arrays, *after)


def project_kernel(first, parts, slot_ref, *refs):
    sides = [
        jnp.concatenate([ref[...] for ref in refs[side * TILES : (side + 1) * TILES]], axis=1)
        for side in range(2)
    ]
    refs = refs[2 * TILES :]
    weights, (out_ref, token_ref) = refs[: sum(parts)], refs[-2:]
    token_ref[...] = jnp.zeros(token_ref.shape, F32)
    at = 0
    for piece, count in enumerate(parts):
        for side, tokens in enumerate(sides):
            result = None
            low = 0
            for part in weights[at : at + count]:
                depth = part.shape[0]
                term = jnp.dot(tokens[:, low : low + depth], part[...], preferred_element_type=F32)
                result = term if result is None else result + term
                low += depth
            out_ref[piece ^ slot_ref[0] if first else 0, side] = result.astype(BF16)
        at += count


def project_part(slot, own, other, pieces, column, width, weight, out, count, after):
    rows, depth = own[0].shape
    parts = [len(piece) for piece in pieces]
    weights = [part for piece in pieces for part in piece]
    steps = 2
    tile = rows // steps
    in_specs = [pl.BlockSpec((tile, depth), lambda i, slot_ref: (i, 0))] * (2 * TILES)
    for i, part in enumerate(weights):
        if i == 0 and out is None:
            in_specs.append(
                pl.BlockSpec(
                    (pl.Element(part.shape[0]), pl.Element(width)), lambda i, slot_ref: (0, column)
                )
            )
        else:
            in_specs.append(pl.BlockSpec(part.shape, lambda i, slot_ref: (0, 0)))
    args = [*own, *other, *weights, *after]
    in_specs += [ANY_SPEC] * len(after)
    aliases = {}
    if out is None:
        out_spec = pl.BlockSpec((count, 2, tile, width), lambda i, slot_ref: (0, 0, i, 0))
    else:
        out_spec = pl.BlockSpec(
            (1, 2, tile, width), lambda i, slot_ref: ((count - 1) ^ slot_ref[0], 0, i, 0)
        )
        aliases = {1 + len(args): 0}
        in_specs.append(ANY_SPEC)
        args.append(out)
    return pl.pallas_call(
        functools.partial(project_kernel, out is None, parts),
        grid_spec=pltpu.PrefetchScalarGridSpec(
            num_scalar_prefetch=1,
            grid=(steps,),
            in_specs=in_specs,
            out_specs=[out_spec, pl.BlockSpec((SUB, LANES), lambda i, slot_ref: (0, 0))],
        ),
        out_shape=[
            jax.ShapeDtypeStruct((count, 2, rows, width), BF16),
            jax.ShapeDtypeStruct((SUB, LANES), F32),
        ],
        input_output_aliases=aliases,
        compiler_params=params(),
        cost_estimate=cost(weight, 8),
        name="project",
    )(slot, *args)


def place_kernel(side_ref, *refs):
    refs[-1][...] = refs[0][...]


def place_both_kernel(side_ref, sums_ref, *refs):
    refs[-2][...] = sums_ref[0]
    refs[-1][...] = sums_ref[1]


def place_part(side, sums, landed, first, out, shape):
    rows, half = shape[0], shape[1] // 2 // LANES
    strip = sums if landed is None else landed
    width = strip.shape[-1]

    def column(i, side_ref):
        which = side_ref[0] if landed is None else 1 - side_ref[0]
        return (0, which * half + first // LANES + i)

    if landed is None:
        in_specs = [pl.BlockSpec((2, rows, LANES), lambda i, side_ref: (0, 0, i))]
    else:
        in_specs = [pl.BlockSpec((rows, LANES), lambda i, side_ref: (0, i))]
    out_specs = [pl.BlockSpec((rows, LANES), column)]
    out_shape = [jax.ShapeDtypeStruct(shape, BF16)]
    if landed is None:
        out_specs.append(pl.BlockSpec((rows, LANES), lambda i, side_ref: (0, i)))
        out_shape.append(jax.ShapeDtypeStruct((rows, width), BF16))
    args, aliases = [strip], {}
    if out is not None:
        aliases = {2: 0}
        in_specs.append(ANY_SPEC)
        args.append(out)
    return pl.pallas_call(
        place_both_kernel if landed is None else place_kernel,
        grid_spec=pltpu.PrefetchScalarGridSpec(
            num_scalar_prefetch=1,
            grid=(width // LANES,),
            in_specs=in_specs,
            out_specs=out_specs,
        ),
        out_shape=out_shape,
        input_output_aliases=aliases,
        compiler_params=params(),
        cost_estimate=cost(0.2, 8),
        name="place",
    )(side, *args)


def body(projected, short_weight, rates, residues, bias, out_weight):
    rows, width = projected.shape[1:]
    depth, columns = out_weight.shape
    count = lax.axis_size("ctx")
    groups = lax.axis_size("ch")
    per = count // groups
    assert per == 2
    mine = lax.axis_index("ctx")
    slot = ((mine // per) ^ lax.axis_index("ch")).astype(jnp.int32)[None]
    near, far = 2, 4
    more = [1 << b for b in range(3, 16) if 1 << b < count]

    units = columns // LANES
    first = max(units // 4, 1)
    second = (units - first + 1) // 2
    widths = [LANES * part for part in (first, second, units - first - second)]
    starts = [sum(widths[:s]) for s in range(len(widths))]
    stages = len(widths)

    def cut_of(s):
        return (out_weight, (0, depth), (starts[s], widths[s]))

    def first_hops(sent):
        return swap(sent, "ctx", near), swap(sent, "ctx", far)

    def second_hops(s, arrived, after, then=True):
        half, cols = depth // 2, (0, widths[s])
        sources = [(arrived[0], (0, half), cols), (arrived[1], (half, half), cols)]
        if then and s + 1 < stages:
            sources.append(cut_of(s + 1))
        low, high, *sent = copy_part(sources, after, "pass_weights")
        diagonal = [swap(low, "ctx", far), swap(high, "ctx", near)]
        return low, diagonal, first_hops(sent[0]) if sent else None

    def pieces_of(s, arrived, diagonal):
        pieces = {
            0: [out_weight],
            near: [arrived[0]],
            far: [arrived[1]],
            near | far: list(diagonal),
        }
        for mask in more:
            for r, parts in list(pieces.items()):
                if r == 0:
                    parts = [out_weight[:, starts[s] : starts[s] + widths[s]]]
                pieces[r ^ mask] = [swap(part, "ctx", mask) for part in parts]
        return [pieces[r] for r in sorted(pieces)]

    last = projected[:, rows - 2 :, :]
    halo = from_behind(last, "ctx")
    (sent,) = copy_part([cut_of(0)], [last], "cut")
    arrived = first_hops(sent)
    y, entry, end = local_part(projected, halo, short_weight, rates, residues, bias[None], sent)
    ends = lax.all_gather(join_part(end, arrived), "ctx")
    token, diagonal, _ = second_hops(0, arrived, [ends], then=False)
    early = TILES - 1
    *mixed, sent = mix_part(
        mine.astype(jnp.int32)[None], projected, halo, short_weight, rates, y, entry, ends,
        range(early), (out_weight, starts[1], widths[1]), [token],
    )
    upcoming = first_hops(sent)
    mixed += mix_part(
        mine.astype(jnp.int32)[None], projected, halo, short_weight, rates, y, entry, ends,
        range(early, TILES), None, [sent, *diagonal],
    )
    other = [swap(part, "ctx", 1) for part in mixed]
    token = mixed[-1]
    slot = (mine // per).astype(jnp.int32)[None]
    side = (mine % per).astype(jnp.int32)[None]
    shape = (rows, per * columns)
    sums = []

    def place_stage(s, out):
        out, given = place_part(side, sums[s], None, starts[s], out, shape)
        return place_part(side, None, swap(given, "ctx", 1), starts[s], out, shape)[0]

    for s in range(stages):
        if s > 0:
            arrived = upcoming
            token, diagonal, upcoming = second_hops(s, arrived, [token, *sums[: s - 1]])
        pieces = pieces_of(s, arrived, diagonal)
        weight = (PA, PB, PC)[s]
        if s == 0:
            partial, token = project_part(
                slot, mixed, other, pieces, starts[s], widths[s], weight, None, groups, [token]
            )
        else:
            partial, token = project_part(
                slot, mixed, other, pieces[:-1], starts[s], widths[s], 0.1, None, groups, [token]
            )
            partial, token = project_part(
                slot, mixed, other, pieces[-1:], starts[s], widths[s], weight, partial, groups, [token]
            )
        if s == stages - 1:
            out = place_stage(0, None)
            partial = join_part(partial, [sums[-1], out])
        elif s > 0:
            partial = join_part(partial, sums[-1:])
        sums.append(lax.psum_scatter(partial, "ch", scatter_dimension=0))
    for s in range(1, stages):
        out = place_stage(s, out)
    return out


def solution(mesh):
    in_specs = (
        P(None, "ctx", "ch"),
        P(None, None, "ch"),
        P(None, "ch"),
        P(None, "ch"),
        P("ch"),
        P("ch", "ctx"),
    )
    out_specs = P("ctx", "ch")
    return jax.shard_map(body, mesh=mesh, in_specs=in_specs, out_specs=out_specs, check_vma=False)
```

```python
import functools

import jax
import jax.numpy as jnp
from jax import lax
from jax.experimental import pallas as pl
from jax.experimental.pallas import tpu as pltpu
from jax.sharding import PartitionSpec as P

F32 = jnp.float32
BF16 = jnp.bfloat16
STEPS = 2
TILES = 4
REACHES = (1, 2, 4)
SUB = 8
LANES = 128
CUTS = 4
K1COST = 60
MIXCOST = 20
PA, PB, PC = 0.1, 35, 40
VMEM = 63 * 1024 * 1024
SMEM_SPEC = pl.BlockSpec(memory_space=pltpu.SMEM)
ANY_SPEC = pl.BlockSpec(memory_space=pl.ANY)


def swap(value, axis, mask):
    count = lax.axis_size(axis)
    return lax.ppermute(value, axis, [(i, i ^ mask) for i in range(count)])


def from_behind(value, axis):
    count = lax.axis_size(axis)
    return lax.ppermute(value, axis, [(i, i + 1) for i in range(count - 1)])


def spread(row):
    return jnp.broadcast_to(row, (SUB, LANES))


def total(parts):
    parts = list(parts)
    while len(parts) > 1:
        parts = [
            parts[i] + parts[i + 1] if i + 1 < len(parts) else parts[i]
            for i in range(0, len(parts), 2)
        ]
    return parts[0]


def rounded(value):
    return value.astype(BF16).astype(F32)


def cost(micros, moved):
    return pl.CostEstimate(flops=int(micros * 1.0e9), bytes_accessed=int(moved), transcendentals=0)


def params():
    return pltpu.CompilerParams(vmem_limit_bytes=VMEM)


def local_kernel(
    k_ref, v_ref, halo_ref, taps_ref, rates_ref, residues_ref, bias_ref, after_ref,
    y_ref, entry_ref, end_ref, k_rows, v_rows, ends,
):
    rows, width = k_ref.shape[1], k_ref.shape[2]
    order = rates_ref.shape[0]
    length = rows // SUB
    unroll = min(8, length)
    sub = lax.broadcasted_iota(jnp.int32, (SUB, LANES), 0)

    def group(index, _):
        lanes = pl.ds(pl.multiple_of(index * LANES, LANES), LANES)
        k_rows[pl.ds(SUB - 2, 2), :] = halo_ref[1, :, lanes].astype(F32)
        v_rows[pl.ds(SUB - 2, 2), :] = halo_ref[2, :, lanes].astype(F32)
        k_rows[pl.ds(SUB, rows), :] = k_ref[0, :, lanes].astype(F32)
        v_rows[pl.ds(SUB, rows), :] = v_ref[0, :, lanes].astype(F32)
        rates = rates_ref[:, lanes]
        all_decay = jnp.exp(-rates)
        all_coef = residues_ref[:, lanes] * jnp.sqrt(2.0 * rates)
        decay = [spread(all_decay[m : m + 1, :]) for m in range(order)]
        coef = [spread(all_coef[m : m + 1, :]) for m in range(order)]
        bias = spread(bias_ref[0:1, lanes])
        kt = [spread(taps_ref[1, j : j + 1, lanes]) for j in range(3)]
        vt = [spread(taps_ref[2, j : j + 1, lanes]) for j in range(3)]

        def pick(ref, b):
            return ref[pl.ds(SUB + b, SUB, stride=length), :]

        def steps(outer, carry):
            k1, k2, v1, v2, state = carry
            for u in range(unroll):
                b = outer * unroll + u
                k0, v0 = pick(k_rows, b), pick(v_rows, b)
                short_k = kt[0] * k0 + kt[1] * k1 + kt[2] * k2
                short_v = vt[0] * v0 + vt[1] * v1 + vt[2] * v2
                gated = rounded(short_k * short_v)
                state = [decay[m] * state[m] + coef[m] * gated for m in range(order)]
                y_ref[b, :, lanes] = total(state + [bias * gated])
                k1, k2, v1, v2 = k0, k1, v0, v1
            return k1, k2, v1, v2, state

        zero = jnp.zeros((SUB, LANES), F32)
        start = (pick(k_rows, -1), pick(k_rows, -2), pick(v_rows, -1), pick(v_rows, -2), [zero] * order)
        state = lax.fori_loop(0, length // unroll, steps, start)[4]
        leaps = {reach: jnp.exp(rates * float(-length * reach)) for reach in REACHES}
        for m in range(order):
            scan = state[m]
            for reach in REACHES:
                earlier = pltpu.roll(scan, reach, 0) * spread(leaps[reach][m : m + 1, :])
                scan = scan + jnp.where(sub >= reach, earlier, 0.0)
            entry_ref[m, :, lanes] = jnp.where(sub >= 1, pltpu.roll(scan, 1, 0), 0.0)
            ends[m : m + 1, :] = scan[SUB - 1 :, :]
        end_ref[:, lanes] = ends[...].astype(end_ref.dtype)
        return 0

    lax.fori_loop(0, width // LANES, group, 0)


def local_part(projected, halo, taps, rates, residues, bias, after):
    rows, width = projected.shape[1:]
    order = rates.shape[0]
    tile = width // TILES
    length = rows // SUB
    return pl.pallas_call(
        local_kernel,
        grid=(width // tile,),
        in_specs=[
            pl.BlockSpec((1, rows, tile), lambda c: (1, 0, c)),
            pl.BlockSpec((1, rows, tile), lambda c: (2, 0, c)),
            pl.BlockSpec((3, 2, tile), lambda c: (0, 0, c)),
            pl.BlockSpec((3, 3, tile), lambda c: (0, 0, c)),
            pl.BlockSpec((order, tile), lambda c: (0, c)),
            pl.BlockSpec((order, tile), lambda c: (0, c)),
            pl.BlockSpec((1, tile), lambda c: (0, c)),
            ANY_SPEC,
        ],
        out_specs=[
            pl.BlockSpec((length, SUB, tile), lambda c: (0, 0, c)),
            pl.BlockSpec((order, SUB, tile), lambda c: (0, 0, c)),
            pl.BlockSpec((order, tile), lambda c: (0, c)),
        ],
        out_shape=[
            jax.ShapeDtypeStruct((length, SUB, width), F32),
            jax.ShapeDtypeStruct((order, SUB, width), F32),
            jax.ShapeDtypeStruct((order, width), BF16),
        ],
        scratch_shapes=[
            pltpu.VMEM((rows + SUB, LANES), F32),
            pltpu.VMEM((rows + SUB, LANES), F32),
            pltpu.VMEM((order, LANES), F32),
        ],
        compiler_params=params(),
        cost_estimate=cost(K1COST, 12 * rows * width),
        name="local_conv",
    )(projected, projected, halo, taps, rates, residues, bias, after)


def mix_kernel(
    cut, mine_ref, q_ref, halo_ref, taps_ref, rates_ref, y_ref, entry_ref, ends_ref, *refs
):
    out, (q_rows, mixed_rows) = refs[-3 - cut], refs[-2:]
    if cut:
        refs[-3][...] = refs[0][...]
    rows, width = q_ref.shape[1], q_ref.shape[2]
    order = rates_ref.shape[0]
    length = rows // SUB
    unroll = min(8, length)
    sub = lax.broadcasted_iota(jnp.int32, (SUB, LANES), 0)

    def group(index, _):
        lanes = pl.ds(pl.multiple_of(index * LANES, LANES), LANES)
        rates = rates_ref[:, lanes]
        across = jnp.exp(-rates * float(rows))
        before = jnp.zeros((order, LANES), F32)
        for device in range(ends_ref.shape[0] - 1):
            later = before * across + ends_ref[device, :, lanes].astype(F32)
            before = jnp.where(device < mine_ref[0], later, before)
        q_rows[pl.ds(SUB - 2, 2), :] = halo_ref[0, :, lanes].astype(F32)
        q_rows[pl.ds(SUB, rows), :] = q_ref[0, :, lanes].astype(F32)
        decay, carried = [], []
        all_decay = jnp.exp(-rates)
        leaps = {reach: jnp.exp(rates * float(-length * reach)) for reach in REACHES}
        for m in range(order):
            decay.append(spread(all_decay[m : m + 1, :]))
            passed = spread(before[m : m + 1, :])
            for reach in REACHES:
                passed = jnp.where(sub & reach == 0, passed, passed * spread(leaps[reach][m : m + 1, :]))
            carried.append((entry_ref[m, :, lanes] + passed) * decay[m])
        qt = [spread(taps_ref[0, j : j + 1, lanes]) for j in range(3)]

        def pick(b):
            return q_rows[pl.ds(SUB + b, SUB, stride=length), :]

        def steps(outer, carry):
            q1, q2, carried = carry
            for u in range(unroll):
                b = outer * unroll + u
                q0 = pick(b)
                short_q = qt[0] * q0 + qt[1] * q1 + qt[2] * q2
                conv = y_ref[b, :, lanes] + total(carried)
                mixed_rows[pl.ds(b, SUB, stride=length), :] = short_q * conv
                carried = [carried[m] * decay[m] for m in range(order)]
                q1, q2 = q0, q1
            return q1, q2, carried

        lax.fori_loop(0, length // unroll, steps, (pick(-1), pick(-2), carried))
        out[:, lanes] = mixed_rows[...].astype(out.dtype)
        return 0

    lax.fori_loop(0, width // LANES, group, 0)


def mix_part(mine, projected, halo, taps, rates, y, entry, ends, tiles, cut, after):
    rows, width = projected.shape[1:]
    order = rates.shape[0]
    tile = width // TILES
    length = rows // SUB
    first, count = tiles[0], len(tiles)
    in_specs = [
        SMEM_SPEC,
        pl.BlockSpec((1, rows, tile), lambda c: (0, 0, first + c)),
        pl.BlockSpec((3, 2, tile), lambda c: (0, 0, first + c)),
        pl.BlockSpec((3, 3, tile), lambda c: (0, 0, first + c)),
        pl.BlockSpec((order, tile), lambda c: (0, first + c)),
        pl.BlockSpec((length, SUB, tile), lambda c: (0, 0, first + c)),
        pl.BlockSpec((order, SUB, tile), lambda c: (0, 0, first + c)),
        pl.BlockSpec((ends.shape[0], order, tile), lambda c: (0, 0, first + c)),
    ]
    out_specs = [pl.BlockSpec((rows, tile), lambda c: (0, c))]
    out_shape = [jax.ShapeDtypeStruct((rows, count * tile), BF16)]
    args = [mine, projected, halo, taps, rates, y, entry, ends]
    if cut:
        w, column, columns = cut
        depth = w.shape[0] // STEPS
        in_specs.append(
            pl.BlockSpec(
                (pl.Element(depth), pl.Element(columns)),
                lambda c: (jnp.minimum(c, STEPS - 1) * depth, column),
            )
        )
        out_specs.append(pl.BlockSpec((depth, columns), lambda c: (jnp.minimum(c, STEPS - 1), 0)))
        out_shape.append(jax.ShapeDtypeStruct((w.shape[0], columns), BF16))
        args.append(w)
    return pl.pallas_call(
        functools.partial(mix_kernel, cut is not None),
        grid=(count,),
        in_specs=in_specs + [ANY_SPEC] * len(after),
        out_specs=out_specs,
        out_shape=out_shape,
        scratch_shapes=[
            pltpu.VMEM((rows + SUB, LANES), F32),
            pltpu.VMEM((rows, LANES), F32),
        ],
        compiler_params=params(),
        cost_estimate=cost(MIXCOST, 8),
        name="mix",
    )(*args, *after)


def join_kernel(*refs):
    pass


def join_part(value, after):
    return pl.pallas_call(
        join_kernel,
        in_specs=[ANY_SPEC] * (1 + len(after)),
        out_specs=ANY_SPEC,
        out_shape=jax.ShapeDtypeStruct(value.shape, value.dtype),
        input_output_aliases={0: 0},
        cost_estimate=cost(0.1, 8),
        name="join",
    )(value, *after)


def copy_kernel(places, *refs):
    count = len(places)
    outs, stages, sems = refs[-2 * count - 1 : -count - 1], refs[-count - 1 : -1], refs[-1]
    moves = []
    for i, (rows, cols) in enumerate(places):
        size = rows[1] // CUTS
        for j in range(CUTS):
            here = pl.ds(j * size, size)
            there = refs[i].at[pl.ds(rows[0] + j * size, size), pl.ds(*cols)]
            moves.append((
                pltpu.make_async_copy(there, stages[i].at[here], sems.at[0, i, j]),
                pltpu.make_async_copy(stages[i].at[here], outs[i].at[here], sems.at[1, i, j]),
            ))
    for load, _ in moves:
        load.start()
    for load, store in moves:
        load.wait()
        store.start()
    for _, store in moves:
        store.wait()


def copy_part(sources, after, name):
    arrays = [array for array, _, _ in sources]
    places = [(rows, cols) for _, rows, cols in sources]
    out_shape = [jax.ShapeDtypeStruct((rows[1], cols[1]), a.dtype) for a, rows, cols in sources]
    return pl.pallas_call(
        functools.partial(copy_kernel, places),
        in_specs=[ANY_SPEC] * (len(arrays) + len(after)),
        out_specs=[ANY_SPEC] * len(out_shape),
        out_shape=out_shape,
        scratch_shapes=[pltpu.VMEM((rows[1], cols[1]), a.dtype) for a, rows, cols in sources]
        + [pltpu.SemaphoreType.DMA((2, len(sources), CUTS))],
        compiler_params=params(),
        cost_estimate=cost(0.1, 8),
        name=name,
    )(*arrays, *after)


def project_kernel(first, groups, parts, sides, slot_ref, *refs):
    out_ref, token_ref = refs[-2:]
    token_ref[...] = jnp.zeros(token_ref.shape, F32)
    refs = iter(refs)
    tokens = [jnp.concatenate([next(refs)[...] for _ in range(count)], axis=1) for count in groups]
    weights = [[[next(refs) for _ in range(count)] for count in piece] for piece in parts]
    for piece in range(len(parts[0])):
        for side, (which, whose) in enumerate(sides):
            result = None
            low = 0
            for part in weights[whose][piece]:
                depth = part.shape[0]
                term = jnp.dot(tokens[which][:, low : low + depth], part[...], preferred_element_type=F32)
                result = term if result is None else result + term
                low += depth
            out_ref[piece ^ slot_ref[0] if first else 0, side] = result.astype(BF16)


def project_part(slot, tokens, weights, column, width, weight, out, count, after):
    sides = [(0, 0), (len(tokens) - 1, len(weights) - 1)]
    rows = tokens[0][0].shape[0]
    steps = 2
    tile = rows // steps
    in_specs = [
        pl.BlockSpec((tile, part.shape[1]), lambda i, slot_ref: (i, 0)) for group in tokens for part in group
    ]
    flat = [part for pieces in weights for piece in pieces for part in piece]
    for i, part in enumerate(flat):
        if i == 0 and out is None:
            in_specs.append(
                pl.BlockSpec(
                    (pl.Element(part.shape[0]), pl.Element(width)), lambda i, slot_ref: (0, column)
                )
            )
        else:
            in_specs.append(pl.BlockSpec(part.shape, lambda i, slot_ref: (0, 0)))
    args = [*(part for group in tokens for part in group), *flat, *after]
    in_specs += [ANY_SPEC] * len(after)
    aliases = {}
    if out is None:
        out_spec = pl.BlockSpec((count, 2, tile, width), lambda i, slot_ref: (0, 0, i, 0))
    else:
        out_spec = pl.BlockSpec(
            (1, 2, tile, width), lambda i, slot_ref: ((count - 1) ^ slot_ref[0], 0, i, 0)
        )
        aliases = {1 + len(args): 0}
        in_specs.append(ANY_SPEC)
        args.append(out)
    groups = [len(group) for group in tokens]
    parts = [[len(piece) for piece in pieces] for pieces in weights]
    return pl.pallas_call(
        functools.partial(project_kernel, out is None, groups, parts, sides),
        grid_spec=pltpu.PrefetchScalarGridSpec(
            num_scalar_prefetch=1,
            grid=(steps,),
            in_specs=in_specs,
            out_specs=[out_spec, pl.BlockSpec((SUB, LANES), lambda i, slot_ref: (0, 0))],
        ),
        out_shape=[
            jax.ShapeDtypeStruct((count, 2, rows, width), BF16),
            jax.ShapeDtypeStruct((SUB, LANES), F32),
        ],
        input_output_aliases=aliases,
        compiler_params=params(),
        cost_estimate=cost(weight, 8),
        name="project",
    )(slot, *args)


def place_kernel(side_ref, *refs):
    refs[-1][...] = refs[0][...]


def place_both_kernel(side_ref, sums_ref, *refs):
    refs[-2][...] = sums_ref[0]
    refs[-1][...] = sums_ref[1]


def place_part(side, sums, landed, first, out, shape):
    rows, half = shape[0], shape[1] // 2 // LANES
    strip = sums if landed is None else landed
    width = strip.shape[-1]

    def column(i, side_ref):
        which = side_ref[0] if landed is None else 1 - side_ref[0]
        return (0, pl.multiple_of((which * half + first // LANES) * LANES, LANES))

    if landed is None:
        in_specs = [pl.BlockSpec((2, rows, width), lambda i, side_ref: (0, 0, 0))]
    else:
        in_specs = [pl.BlockSpec((rows, width), lambda i, side_ref: (0, 0))]
    out_specs = [pl.BlockSpec((pl.Element(rows), pl.Element(width)), column)]
    out_shape = [jax.ShapeDtypeStruct(shape, BF16)]
    if landed is None:
        out_specs.append(pl.BlockSpec((rows, width), lambda i, side_ref: (0, 0)))
        out_shape.append(jax.ShapeDtypeStruct((rows, width), BF16))
    args, aliases = [strip], {}
    if out is not None:
        aliases = {2: 0}
        in_specs.append(ANY_SPEC)
        args.append(out)
    return pl.pallas_call(
        place_both_kernel if landed is None else place_kernel,
        grid_spec=pltpu.PrefetchScalarGridSpec(
            num_scalar_prefetch=1,
            grid=(1,),
            in_specs=in_specs,
            out_specs=out_specs,
        ),
        out_shape=out_shape,
        input_output_aliases=aliases,
        compiler_params=params(),
        cost_estimate=cost(0.2, 8),
        name="place",
    )(side, *args)


def place_last_kernel(side_ref, sums_ref, *refs):
    refs[-1][...] = sums_ref[0]


def place_last(side, sums, first, out):
    rows, half = out.shape[0], out.shape[1] // 2 // LANES
    width = sums.shape[-1]

    def column(i, side_ref):
        which = side_ref[0] ^ i
        return (0, pl.multiple_of((which * half + first // LANES) * LANES, LANES))

    return pl.pallas_call(
        place_last_kernel,
        grid_spec=pltpu.PrefetchScalarGridSpec(
            num_scalar_prefetch=1,
            grid=(2,),
            in_specs=[pl.BlockSpec((1, rows, width), lambda i, side_ref: (i, 0, 0)), ANY_SPEC],
            out_specs=pl.BlockSpec((pl.Element(rows), pl.Element(width)), column),
        ),
        out_shape=jax.ShapeDtypeStruct(out.shape, BF16),
        input_output_aliases={2: 0},
        compiler_params=params(),
        cost_estimate=cost(0.2, 8),
        name="place",
    )(side, sums, out)


def body(projected, short_weight, rates, residues, bias, out_weight):
    rows, width = projected.shape[1:]
    depth, columns = out_weight.shape
    count = lax.axis_size("ctx")
    groups = lax.axis_size("ch")
    per = count // groups
    assert per == 2
    mine = lax.axis_index("ctx")
    slot = ((mine // per) ^ lax.axis_index("ch")).astype(jnp.int32)[None]
    near, far = 2, 4
    more = [1 << b for b in range(3, 16) if 1 << b < count]

    units = columns // LANES
    first = max(units // 4, 1)
    second = (units - first + 1) // 2
    widths = [LANES * part for part in (first, second, units - first - second)]
    starts = [sum(widths[:s]) for s in range(len(widths))]
    stages = len(widths)

    def cut_of(s):
        return (out_weight, (0, depth), (starts[s], widths[s]))

    def first_hops(sent):
        return swap(sent, "ctx", near), swap(sent, "ctx", far)

    def second_hops(s, arrived, after):
        half, cols = depth // 2, (0, widths[s])
        sources = [(arrived[0], (0, half), cols), (arrived[1], (half, half), cols)]
        if s + 1 < stages:
            sources.append(cut_of(s + 1))
        low, high, *sent = copy_part(sources, after, "pass_weights")
        diagonal = [swap(low, "ctx", far), swap(high, "ctx", near)]
        return low, diagonal, sent[0] if sent else None

    def pieces_of(s, arrived, diagonal):
        pieces = {
            0: [out_weight],
            near: arrived[0] if isinstance(arrived[0], list) else [arrived[0]],
            far: arrived[1] if isinstance(arrived[1], list) else [arrived[1]],
            near | far: list(diagonal),
        }
        for mask in more:
            for r, parts in list(pieces.items()):
                if r == 0:
                    parts = [out_weight[:, starts[s] : starts[s] + widths[s]]]
                pieces[r ^ mask] = [swap(part, "ctx", mask) for part in parts]
        return [pieces[r] for r in sorted(pieces)]

    last = projected[:, rows - 2 :, :]
    sent = copy_part(
        [(out_weight, (top, depth // 2), (starts[0], widths[0])) for top in (0, depth // 2)], [last], "cut"
    )
    halo = from_behind(join_part(last, sent), "ctx")
    hops = [swap(part, "ctx", mask) for mask in (near, far) for part in sent]
    y, entry, end = local_part(projected, halo, short_weight, rates, residues, bias[None], sent[0])
    ends = lax.all_gather(join_part(end, hops), "ctx")
    low_top = join_part(hops[0], [ends])
    high_bottom = join_part(hops[3], [ends])
    diagonal = [swap(low_top, "ctx", far), swap(high_bottom, "ctx", near)]
    arrived = [[low_top, hops[1]], [hops[2], high_bottom]]
    early = TILES - 1
    *mixed, sent = mix_part(
        mine.astype(jnp.int32)[None], projected, halo, short_weight, rates, y, entry, ends,
        range(early), (out_weight, starts[1], widths[1]), [],
    )
    upcoming = first_hops(sent)
    mixed += mix_part(
        mine.astype(jnp.int32)[None], projected, halo, short_weight, rates, y, entry, ends,
        range(early, TILES), None, [sent, *diagonal],
    )
    other = [swap(part, "ctx", 1) for part in mixed]
    token = mixed[-1]
    slot = (mine // per).astype(jnp.int32)[None]
    side = (mine % per).astype(jnp.int32)[None]
    shape = (rows, per * columns)
    sums = []

    def place_stage(s, out):
        out, given = place_part(side, sums[s], None, starts[s], out, shape)
        return place_part(side, None, swap(given, "ctx", 1), starts[s], out, shape)[0]

    for s in range(stages):
        if s > 0:
            arrived, cut = upcoming, sent
            token, diagonal, sent = second_hops(s, arrived, [token, *sums[: s - 1]])
            upcoming = first_hops(sent) if s + 1 < stages else None
        if s > 0 and s + 1 == stages:
            arrived = [join_part(part, [token]) for part in arrived]
            cut = join_part(cut, [token])
        pieces = pieces_of(s, arrived, diagonal)
        weight = (PA, PB, PC)[s]
        if s + 1 < stages:
            tokens, weights = [mixed, other], [pieces]
        else:
            theirs = [[swap(part, "ctx", 1) for part in piece] for piece in [[cut], *pieces[1:-1]]]
            tokens, weights = [mixed], [pieces, [*theirs, None]]
        if s == 0:
            partial, token = project_part(
                slot, tokens, weights, starts[s], widths[s], weight, None, groups, [token]
            )
        else:
            partial, token = project_part(
                slot, tokens, [part[:-1] for part in weights], starts[s], widths[s], 0.1, None, groups, [token]
            )
            if s + 1 == stages:
                held = [join_part(part, [token]) for part in pieces[-1]]
                weights = [[held], [[swap(part, "ctx", 1) for part in held]]]
            partial, token = project_part(
                slot, tokens, [part[-1:] for part in weights], starts[s], widths[s], weight, partial, groups, [token]
            )
        if s > 0:
            partial = join_part(partial, sums[-1:])
        sums.append(lax.psum_scatter(partial, "ch", scatter_dimension=0))
    out = None
    for s in range(stages - 1):
        out = place_stage(s, out)
    return place_last(side, sums[-1], starts[-1], out)


def solution(mesh):
    in_specs = (
        P(None, "ctx", "ch"),
        P(None, None, "ch"),
        P(None, "ch"),
        P(None, "ch"),
        P("ch"),
        P("ch", "ctx"),
    )
    out_specs = P("ctx", "ch")
    return jax.shard_map(body, mesh=mesh, in_specs=in_specs, out_specs=out_specs, check_vma=False)
```

```python
import functools

import jax
import jax.numpy as jnp
from jax import lax
from jax.experimental import pallas as pl
from jax.experimental.pallas import tpu as pltpu
from jax.sharding import PartitionSpec as P

F32 = jnp.float32
BF16 = jnp.bfloat16
STEPS = 2
TILES = 8
REACHES = (1, 2, 4)
SUB = 8
LANES = 128
CUTS = 4
K1COST = 60
MIXCOST = 20
PA, PB, PC = 0.1, 35, 40
VMEM = 63 * 1024 * 1024
SMEM_SPEC = pl.BlockSpec(memory_space=pltpu.SMEM)
ANY_SPEC = pl.BlockSpec(memory_space=pl.ANY)


def swap(value, axis, mask):
    count = lax.axis_size(axis)
    return lax.ppermute(value, axis, [(i, i ^ mask) for i in range(count)])


def from_behind(value, axis):
    count = lax.axis_size(axis)
    return lax.ppermute(value, axis, [(i, (i + 1) % count) for i in range(count)])


def spread(row):
    return jnp.broadcast_to(row, (SUB, LANES))


def total(parts):
    parts = list(parts)
    while len(parts) > 1:
        parts = [
            parts[i] + parts[i + 1] if i + 1 < len(parts) else parts[i]
            for i in range(0, len(parts), 2)
        ]
    return parts[0]


def rounded(value):
    return value.astype(BF16).astype(F32)


def cost(micros, moved):
    return pl.CostEstimate(flops=int(micros * 1.0e9), bytes_accessed=int(moved), transcendentals=0)


def params():
    return pltpu.CompilerParams(vmem_limit_bytes=VMEM)


def local_kernel(
    mine_ref, k_ref, v_ref, halo_ref, taps_ref, rates_ref, residues_ref, bias_ref, after_ref,
    y_ref, entry_ref, end_ref, k_rows, v_rows, ends,
):
    rows, width = k_ref.shape[1], k_ref.shape[2]
    order = rates_ref.shape[0]
    length = rows // SUB
    unroll = min(16, length)
    sub = lax.broadcasted_iota(jnp.int32, (SUB, LANES), 0)

    def group(index, _):
        lanes = pl.ds(pl.multiple_of(index * LANES, LANES), LANES)
        k_rows[pl.ds(SUB - 2, 2), :] = jnp.where(mine_ref[0] > 0, halo_ref[1, :, lanes].astype(F32), 0.0)
        v_rows[pl.ds(SUB - 2, 2), :] = jnp.where(mine_ref[0] > 0, halo_ref[2, :, lanes].astype(F32), 0.0)
        k_rows[pl.ds(SUB, rows), :] = k_ref[0, :, lanes].astype(F32)
        v_rows[pl.ds(SUB, rows), :] = v_ref[0, :, lanes].astype(F32)
        rates = rates_ref[:, lanes]
        all_decay = jnp.exp(-rates)
        all_coef = residues_ref[:, lanes] * jnp.sqrt(2.0 * rates)
        decay = [spread(all_decay[m : m + 1, :]) for m in range(order)]
        coef = [spread(all_coef[m : m + 1, :]) for m in range(order)]
        bias = spread(bias_ref[0:1, lanes])
        kt = [spread(taps_ref[1, j : j + 1, lanes]) for j in range(3)]
        vt = [spread(taps_ref[2, j : j + 1, lanes]) for j in range(3)]

        def pick(ref, b):
            return ref[pl.ds(SUB + b, SUB, stride=length), :]

        def steps(outer, carry):
            k1, k2, v1, v2, state = carry
            for u in range(unroll):
                b = outer * unroll + u
                k0, v0 = pick(k_rows, b), pick(v_rows, b)
                short_k = kt[0] * k0 + kt[1] * k1 + kt[2] * k2
                short_v = vt[0] * v0 + vt[1] * v1 + vt[2] * v2
                gated = rounded(short_k * short_v)
                state = [decay[m] * state[m] + coef[m] * gated for m in range(order)]
                y_ref[b, :, lanes] = total(state + [bias * gated])
                k1, k2, v1, v2 = k0, k1, v0, v1
            return k1, k2, v1, v2, state

        zero = jnp.zeros((SUB, LANES), F32)
        start = (pick(k_rows, -1), pick(k_rows, -2), pick(v_rows, -1), pick(v_rows, -2), [zero] * order)
        state = lax.fori_loop(0, length // unroll, steps, start)[4]
        leaps = {reach: jnp.exp(rates * float(-length * reach)) for reach in REACHES}
        for m in range(order):
            scan = state[m]
            for reach in REACHES:
                earlier = pltpu.roll(scan, reach, 0) * spread(leaps[reach][m : m + 1, :])
                scan = scan + jnp.where(sub >= reach, earlier, 0.0)
            entry_ref[m, :, lanes] = jnp.where(sub >= 1, pltpu.roll(scan, 1, 0), 0.0)
            ends[m : m + 1, :] = scan[SUB - 1 :, :]
        end_ref[:, lanes] = ends[...].astype(end_ref.dtype)
        return 0

    lax.fori_loop(0, width // LANES, group, 0)


def local_part(mine, projected, halo, taps, rates, residues, bias, after):
    rows, width = projected.shape[1:]
    order = rates.shape[0]
    tile = width // TILES
    length = rows // SUB
    return pl.pallas_call(
        local_kernel,
        grid=(width // tile,),
        in_specs=[
            SMEM_SPEC,
            pl.BlockSpec((1, rows, tile), lambda c: (1, 0, c)),
            pl.BlockSpec((1, rows, tile), lambda c: (2, 0, c)),
            pl.BlockSpec((3, 2, tile), lambda c: (0, 0, c)),
            pl.BlockSpec((3, 3, tile), lambda c: (0, 0, c)),
            pl.BlockSpec((order, tile), lambda c: (0, c)),
            pl.BlockSpec((order, tile), lambda c: (0, c)),
            pl.BlockSpec((1, tile), lambda c: (0, c)),
            ANY_SPEC,
        ],
        out_specs=[
            pl.BlockSpec((length, SUB, tile), lambda c: (0, 0, c)),
            pl.BlockSpec((order, SUB, tile), lambda c: (0, 0, c)),
            pl.BlockSpec((order, tile), lambda c: (0, c)),
        ],
        out_shape=[
            jax.ShapeDtypeStruct((length, SUB, width), F32),
            jax.ShapeDtypeStruct((order, SUB, width), F32),
            jax.ShapeDtypeStruct((order, width), BF16),
        ],
        scratch_shapes=[
            pltpu.VMEM((rows + SUB, LANES), F32),
            pltpu.VMEM((rows + SUB, LANES), F32),
            pltpu.VMEM((order, LANES), F32),
        ],
        compiler_params=params(),
        cost_estimate=cost(K1COST, 12 * rows * width),
        name="local_conv",
    )(mine, projected, projected, halo, taps, rates, residues, bias, after)


def mix_kernel(
    cut, mine_ref, q_ref, halo_ref, taps_ref, rates_ref, y_ref, entry_ref, ends_ref, *refs
):
    out, (q_rows, mixed_rows) = refs[-3 - cut], refs[-2:]
    if cut:
        refs[-3][...] = refs[0][...]
    rows, width = q_ref.shape[1], q_ref.shape[2]
    order = rates_ref.shape[0]
    length = rows // SUB
    unroll = min(8, length)
    sub = lax.broadcasted_iota(jnp.int32, (SUB, LANES), 0)

    def group(index, _):
        lanes = pl.ds(pl.multiple_of(index * LANES, LANES), LANES)
        rates = rates_ref[:, lanes]
        across = jnp.exp(-rates * float(rows))
        before = jnp.zeros((order, LANES), F32)
        for device in range(ends_ref.shape[0] - 1):
            later = before * across + ends_ref[device, :, lanes].astype(F32)
            before = jnp.where(device < mine_ref[0], later, before)
        q_rows[pl.ds(SUB - 2, 2), :] = jnp.where(mine_ref[0] > 0, halo_ref[0, :, lanes].astype(F32), 0.0)
        q_rows[pl.ds(SUB, rows), :] = q_ref[0, :, lanes].astype(F32)
        decay, carried = [], []
        all_decay = jnp.exp(-rates)
        leaps = {reach: jnp.exp(rates * float(-length * reach)) for reach in REACHES}
        for m in range(order):
            decay.append(spread(all_decay[m : m + 1, :]))
            passed = spread(before[m : m + 1, :])
            for reach in REACHES:
                passed = jnp.where(sub & reach == 0, passed, passed * spread(leaps[reach][m : m + 1, :]))
            carried.append((entry_ref[m, :, lanes] + passed) * decay[m])
        qt = [spread(taps_ref[0, j : j + 1, lanes]) for j in range(3)]

        def pick(b):
            return q_rows[pl.ds(SUB + b, SUB, stride=length), :]

        def steps(outer, carry):
            q1, q2, carried = carry
            for u in range(unroll):
                b = outer * unroll + u
                q0 = pick(b)
                short_q = qt[0] * q0 + qt[1] * q1 + qt[2] * q2
                conv = y_ref[b, :, lanes] + total(carried)
                mixed_rows[pl.ds(b, SUB, stride=length), :] = short_q * conv
                carried = [carried[m] * decay[m] for m in range(order)]
                q1, q2 = q0, q1
            return q1, q2, carried

        lax.fori_loop(0, length // unroll, steps, (pick(-1), pick(-2), carried))
        out[:, lanes] = mixed_rows[...].astype(out.dtype)
        return 0

    lax.fori_loop(0, width // LANES, group, 0)


def mix_part(mine, projected, halo, taps, rates, y, entry, ends, tiles, cut, after):
    rows, width = projected.shape[1:]
    order = rates.shape[0]
    tile = width // TILES
    length = rows // SUB
    first, count = tiles[0], len(tiles)
    in_specs = [
        SMEM_SPEC,
        pl.BlockSpec((1, rows, tile), lambda c: (0, 0, first + c)),
        pl.BlockSpec((3, 2, tile), lambda c: (0, 0, first + c)),
        pl.BlockSpec((3, 3, tile), lambda c: (0, 0, first + c)),
        pl.BlockSpec((order, tile), lambda c: (0, first + c)),
        pl.BlockSpec((length, SUB, tile), lambda c: (0, 0, first + c)),
        pl.BlockSpec((order, SUB, tile), lambda c: (0, 0, first + c)),
        pl.BlockSpec((ends.shape[0], order, tile), lambda c: (0, 0, first + c)),
    ]
    out_specs = [pl.BlockSpec((rows, tile), lambda c: (0, c))]
    out_shape = [jax.ShapeDtypeStruct((rows, count * tile), BF16)]
    args = [mine, projected, halo, taps, rates, y, entry, ends]
    if cut:
        w, column, columns = cut
        depth = w.shape[0] // STEPS
        in_specs.append(
            pl.BlockSpec(
                (pl.Element(depth), pl.Element(columns)),
                lambda c: (jnp.minimum(c, STEPS - 1) * depth, column),
            )
        )
        out_specs.append(pl.BlockSpec((depth, columns), lambda c: (jnp.minimum(c, STEPS - 1), 0)))
        out_shape.append(jax.ShapeDtypeStruct((w.shape[0], columns), BF16))
        args.append(w)
    return pl.pallas_call(
        functools.partial(mix_kernel, cut is not None),
        grid=(count,),
        in_specs=in_specs + [ANY_SPEC] * len(after),
        out_specs=out_specs,
        out_shape=out_shape,
        scratch_shapes=[
            pltpu.VMEM((rows + SUB, LANES), F32),
            pltpu.VMEM((rows, LANES), F32),
        ],
        compiler_params=params(),
        cost_estimate=cost(MIXCOST, 8),
        name="mix",
    )(*args, *after)


def join_kernel(*refs):
    pass


def join_part(value, after):
    return pl.pallas_call(
        join_kernel,
        in_specs=[ANY_SPEC] * (1 + len(after)),
        out_specs=ANY_SPEC,
        out_shape=jax.ShapeDtypeStruct(value.shape, value.dtype),
        input_output_aliases={0: 0},
        cost_estimate=cost(0.1, 8),
        name="join",
    )(value, *after)


def copy_kernel(places, *refs):
    count = len(places)
    outs, stages, sems = refs[-2 * count - 1 : -count - 1], refs[-count - 1 : -1], refs[-1]
    moves = []
    for i, (rows, cols) in enumerate(places):
        size = rows[1] // CUTS
        for j in range(CUTS):
            here = pl.ds(j * size, size)
            there = refs[i].at[pl.ds(rows[0] + j * size, size), pl.ds(*cols)]
            moves.append((
                pltpu.make_async_copy(there, stages[i].at[here], sems.at[0, i, j]),
                pltpu.make_async_copy(stages[i].at[here], outs[i].at[here], sems.at[1, i, j]),
            ))
    for load, _ in moves:
        load.start()
    for load, store in moves:
        load.wait()
        store.start()
    for _, store in moves:
        store.wait()


def copy_part(sources, after, name):
    arrays = [array for array, _, _ in sources]
    places = [(rows, cols) for _, rows, cols in sources]
    out_shape = [jax.ShapeDtypeStruct((rows[1], cols[1]), a.dtype) for a, rows, cols in sources]
    return pl.pallas_call(
        functools.partial(copy_kernel, places),
        in_specs=[ANY_SPEC] * (len(arrays) + len(after)),
        out_specs=[ANY_SPEC] * len(out_shape),
        out_shape=out_shape,
        scratch_shapes=[pltpu.VMEM((rows[1], cols[1]), a.dtype) for a, rows, cols in sources]
        + [pltpu.SemaphoreType.DMA((2, len(sources), CUTS))],
        compiler_params=params(),
        cost_estimate=cost(0.1, 8),
        name=name,
    )(*arrays, *after)


def project_kernel(first, groups, parts, sides, slot_ref, *refs):
    out_ref, token_ref = refs[-2:]
    token_ref[...] = jnp.zeros(token_ref.shape, F32)
    refs = iter(refs)
    tokens = [jnp.concatenate([next(refs)[...] for _ in range(count)], axis=1) for count in groups]
    weights = [[[next(refs) for _ in range(count)] for count in piece] for piece in parts]
    for piece in range(len(parts[0])):
        for side, (which, whose) in enumerate(sides):
            result = None
            low = 0
            for part in weights[whose][piece]:
                depth = part.shape[0]
                term = jnp.dot(tokens[which][:, low : low + depth], part[...], preferred_element_type=F32)
                result = term if result is None else result + term
                low += depth
            out_ref[piece ^ slot_ref[0] if first else 0, side] = result.astype(BF16)


def project_part(slot, tokens, weights, column, width, weight, out, count, after):
    sides = [(0, 0), (len(tokens) - 1, len(weights) - 1)]
    rows = tokens[0][0].shape[0]
    steps = 2
    tile = rows // steps
    in_specs = [
        pl.BlockSpec((tile, part.shape[1]), lambda i, slot_ref: (i, 0)) for group in tokens for part in group
    ]
    flat = [part for pieces in weights for piece in pieces for part in piece]
    for i, part in enumerate(flat):
        if i == 0 and out is None:
            in_specs.append(
                pl.BlockSpec(
                    (pl.Element(part.shape[0]), pl.Element(width)), lambda i, slot_ref: (0, column)
                )
            )
        else:
            in_specs.append(pl.BlockSpec(part.shape, lambda i, slot_ref: (0, 0)))
    args = [*(part for group in tokens for part in group), *flat, *after]
    in_specs += [ANY_SPEC] * len(after)
    aliases = {}
    if out is None:
        out_spec = pl.BlockSpec((count, 2, tile, width), lambda i, slot_ref: (0, 0, i, 0))
    else:
        out_spec = pl.BlockSpec(
            (1, 2, tile, width), lambda i, slot_ref: ((count - 1) ^ slot_ref[0], 0, i, 0)
        )
        aliases = {1 + len(args): 0}
        in_specs.append(ANY_SPEC)
        args.append(out)
    groups = [len(group) for group in tokens]
    parts = [[len(piece) for piece in pieces] for pieces in weights]
    return pl.pallas_call(
        functools.partial(project_kernel, out is None, groups, parts, sides),
        grid_spec=pltpu.PrefetchScalarGridSpec(
            num_scalar_prefetch=1,
            grid=(steps,),
            in_specs=in_specs,
            out_specs=[out_spec, pl.BlockSpec((SUB, LANES), lambda i, slot_ref: (0, 0))],
        ),
        out_shape=[
            jax.ShapeDtypeStruct((count, 2, rows, width), BF16),
            jax.ShapeDtypeStruct((SUB, LANES), F32),
        ],
        input_output_aliases=aliases,
        compiler_params=params(),
        cost_estimate=cost(weight, 8),
        name="project",
    )(slot, *args)


def place_kernel(side_ref, *refs):
    refs[-1][...] = refs[0][...]


def place_both_kernel(side_ref, sums_ref, *refs):
    refs[-2][...] = sums_ref[0]
    refs[-1][...] = sums_ref[1]


def place_part(side, sums, landed, first, out, shape):
    rows, half = shape[0], shape[1] // 2 // LANES
    strip = sums if landed is None else landed
    width = strip.shape[-1]

    def column(i, side_ref):
        which = side_ref[0] if landed is None else 1 - side_ref[0]
        return (0, pl.multiple_of((which * half + first // LANES) * LANES, LANES))

    if landed is None:
        in_specs = [pl.BlockSpec((2, rows, width), lambda i, side_ref: (0, 0, 0))]
    else:
        in_specs = [pl.BlockSpec((rows, width), lambda i, side_ref: (0, 0))]
    out_specs = [pl.BlockSpec((pl.Element(rows), pl.Element(width)), column)]
    out_shape = [jax.ShapeDtypeStruct(shape, BF16)]
    if landed is None:
        out_specs.append(pl.BlockSpec((rows, width), lambda i, side_ref: (0, 0)))
        out_shape.append(jax.ShapeDtypeStruct((rows, width), BF16))
    args, aliases = [strip], {}
    if out is not None:
        aliases = {2: 0}
        in_specs.append(ANY_SPEC)
        args.append(out)
    return pl.pallas_call(
        place_both_kernel if landed is None else place_kernel,
        grid_spec=pltpu.PrefetchScalarGridSpec(
            num_scalar_prefetch=1,
            grid=(1,),
            in_specs=in_specs,
            out_specs=out_specs,
        ),
        out_shape=out_shape,
        input_output_aliases=aliases,
        compiler_params=params(),
        cost_estimate=cost(0.2, 8),
        name="place",
    )(side, *args)


def place_last_kernel(side_ref, sums_ref, *refs):
    refs[-1][...] = sums_ref[0]


def place_last(side, sums, first, out):
    rows, half = out.shape[0], out.shape[1] // 2 // LANES
    width = sums.shape[-1]

    def column(i, side_ref):
        which = side_ref[0] ^ i
        return (0, pl.multiple_of((which * half + first // LANES) * LANES, LANES))

    return pl.pallas_call(
        place_last_kernel,
        grid_spec=pltpu.PrefetchScalarGridSpec(
            num_scalar_prefetch=1,
            grid=(2,),
            in_specs=[pl.BlockSpec((1, rows, width), lambda i, side_ref: (i, 0, 0)), ANY_SPEC],
            out_specs=pl.BlockSpec((pl.Element(rows), pl.Element(width)), column),
        ),
        out_shape=jax.ShapeDtypeStruct(out.shape, BF16),
        input_output_aliases={2: 0},
        compiler_params=params(),
        cost_estimate=cost(0.2, 8),
        name="place",
    )(side, sums, out)


def body(projected, short_weight, rates, residues, bias, out_weight):
    rows, width = projected.shape[1:]
    depth, columns = out_weight.shape
    count = lax.axis_size("ctx")
    groups = lax.axis_size("ch")
    per = count // groups
    assert per == 2
    mine = lax.axis_index("ctx")
    slot = ((mine // per) ^ lax.axis_index("ch")).astype(jnp.int32)[None]
    near, far = 2, 4
    more = [1 << b for b in range(3, 16) if 1 << b < count]

    units = columns // LANES
    first = max(units // 4, 1)
    second = (units - first + 1) // 2
    widths = [LANES * part for part in (first, second, units - first - second)]
    starts = [sum(widths[:s]) for s in range(len(widths))]
    stages = len(widths)

    def cut_of(s):
        return (out_weight, (0, depth), (starts[s], widths[s]))

    def first_hops(sent):
        return swap(sent, "ctx", near), swap(sent, "ctx", far)

    def second_hops(s, arrived, after):
        half, cols = depth // 2, (0, widths[s])
        sources = [(arrived[0], (0, half), cols), (arrived[1], (half, half), cols)]
        if s + 1 < stages:
            sources.append(cut_of(s + 1))
        low, high, *sent = copy_part(sources, after, "pass_weights")
        diagonal = [swap(low, "ctx", far), swap(high, "ctx", near)]
        return low, diagonal, sent[0] if sent else None

    def pieces_of(s, arrived, diagonal):
        pieces = {
            0: [out_weight],
            near: arrived[0] if isinstance(arrived[0], list) else [arrived[0]],
            far: arrived[1] if isinstance(arrived[1], list) else [arrived[1]],
            near | far: list(diagonal),
        }
        for mask in more:
            for r, parts in list(pieces.items()):
                if r == 0:
                    parts = [out_weight[:, starts[s] : starts[s] + widths[s]]]
                pieces[r ^ mask] = [swap(part, "ctx", mask) for part in parts]
        return [pieces[r] for r in sorted(pieces)]

    last = projected[:, rows - 2 :, :]
    sent = copy_part(
        [(out_weight, (top, depth // 2), (starts[0], widths[0])) for top in (0, depth // 2)], [last], "cut"
    )
    halo = from_behind(join_part(last, sent), "ctx")
    hops = [swap(part, "ctx", mask) for mask in (near, far) for part in sent]
    here = mine.astype(jnp.int32)[None]
    y, entry, end = local_part(here, projected, halo, short_weight, rates, residues, bias[None], sent[0])
    ends = lax.all_gather(join_part(end, hops), "ctx")
    low_top = join_part(hops[0], [ends])
    high_bottom = join_part(hops[3], [ends])
    diagonal = [swap(low_top, "ctx", far), swap(high_bottom, "ctx", near)]
    arrived = [[low_top, hops[1]], [hops[2], high_bottom]]
    early = TILES * 3 // 4
    *mixed, sent = mix_part(
        here, projected, halo, short_weight, rates, y, entry, ends,
        range(early), (out_weight, starts[1], widths[1]), [],
    )
    upcoming = first_hops(sent)
    mixed += mix_part(
        here, projected, halo, short_weight, rates, y, entry, ends,
        range(early, TILES), None, [sent, *diagonal],
    )
    other = [swap(part, "ctx", 1) for part in mixed]
    token = mixed[-1]
    slot = (mine // per).astype(jnp.int32)[None]
    side = (mine % per).astype(jnp.int32)[None]
    shape = (rows, per * columns)
    sums = []

    def place_stage(s, out):
        out, given = place_part(side, sums[s], None, starts[s], out, shape)
        return place_part(side, None, swap(given, "ctx", 1), starts[s], out, shape)[0]

    for s in range(stages):
        if s > 0:
            arrived, cut = upcoming, sent
            token, diagonal, sent = second_hops(s, arrived, [token, *sums[: s - 1]])
            upcoming = first_hops(sent) if s + 1 < stages else None
        if s > 0 and s + 1 == stages:
            arrived = [join_part(part, [token]) for part in arrived]
            cut = join_part(cut, [token])
        pieces = pieces_of(s, arrived, diagonal)
        weight = (PA, PB, PC)[s]
        if s + 1 < stages:
            tokens, weights = [mixed, other], [pieces]
        else:
            theirs = [[swap(part, "ctx", 1) for part in piece] for piece in [[cut], *pieces[1:-1]]]
            tokens, weights = [mixed], [pieces, [*theirs, None]]
        if s == 0:
            partial, token = project_part(
                slot, tokens, weights, starts[s], widths[s], weight, None, groups, [token]
            )
        else:
            partial, token = project_part(
                slot, tokens, [part[:-1] for part in weights], starts[s], widths[s], 0.1, None, groups, [token]
            )
            if s + 1 == stages:
                held = [join_part(part, [token]) for part in pieces[-1]]
                weights = [[held], [[swap(part, "ctx", 1) for part in held]]]
            partial, token = project_part(
                slot, tokens, [part[-1:] for part in weights], starts[s], widths[s], weight, partial, groups, [token]
            )
        if s > 0:
            partial = join_part(partial, sums[-1:])
        sums.append(lax.psum_scatter(partial, "ch", scatter_dimension=0))
    out = None
    for s in range(stages - 1):
        out = place_stage(s, out)
    return place_last(side, sums[-1], starts[-1], out)


def solution(mesh):
    in_specs = (
        P(None, "ctx", "ch"),
        P(None, None, "ch"),
        P(None, "ch"),
        P(None, "ch"),
        P("ch"),
        P("ch", "ctx"),
    )
    out_specs = P("ctx", "ch")
    return jax.shard_map(body, mesh=mesh, in_specs=in_specs, out_specs=out_specs, check_vma=False)
```
